32 devices in a mesh: seq: 8 (over z, y), ch: 4 (over x, core).
Axes of the slice: x: 2, y: 2, z: 4, core: 2. Of those that a mesh axis runs over, the one named last changes fastest.
Arguments:
- stream: bfloat16 [2048, 1536], P('seq', 'ch'), may hold values from -6 to 6
- norm_gain: float32 [9, 1536], replicated, may hold values from 0.25 to 1.75
- conv_weight: bfloat16 [8, 3, 1536, 768], P(None, None, 'seq', 'ch'), may hold values from -0.09375 to 0.09375
- conv_bias: float32 [8, 768], P(None, 'ch'), may hold values from -3 to 3
- point_weight: bfloat16 [8, 768, 1536], P(None, 'seq', 'ch'), may hold values from -0.21875 to 0.21875
- point_bias: float32 [8, 1536], P(None, 'ch'), may hold values from -2 to 2
- head_weight: bfloat16 [1536, 3840], P('seq', 'ch'), may hold values from -0.15625 to 0.15625
- head_bias: float32 [3840], P('ch'), may hold values from -3 to 3
- exon_start: int32 [512], replicated, may hold values from 0 to 2016, as said below
- exon_length: int32 [512], replicated, may hold values from 1 to 32
- exon_transcript: int32 [512], replicated, may hold values from 0 to 63, as said below
- transcript_slot: int32 [64], replicated, may hold values from 0 to 63, each once
Outputs:
- transcript_cov: float32 [64, 3840], P('seq', 'ch')
The draws below stay inside these ranges and needn't reach their ends.
Inputs may be any that keep to these rules, and one draw needn't show every extreme that they name: An exon of transcript t starts in bins t * 32 to t * 32 + 31, and exon_start[e] + exon_length[e] <= 2048. `exon_transcript`: never falls along the exons; every transcript has 1 to 15 exons, one exactly 15; transcripts 2 i and 2 i + 1 together have 2 * 8. `transcript_slot`: each row once.
All inputs are finite; a program needn't handle non-finite values.
Results may differ from the reference program's by a relative error of at most 0.00065.
Values may be sent and summed in bfloat16 or wider, within the bound.
A program may use at most 128 MiB of HBM per device.

```python
import jax
import jax.numpy as jnp
from jax import lax

CH = 1536
HID = 768
TRACKS = 3840
LAYERS = 8
EXONS_TX = 8
MOST_EXONS = 15
SPAN = 32
BINS = 2048
NTX = 64
NEXON = 512


def exon_owner(key):
    pairs = NTX // 2
    first = jax.random.randint(jax.random.fold_in(key, 11), (pairs,), 1, MOST_EXONS + 1).astype(jnp.int32)
    first = first.at[0].set(MOST_EXONS)
    per_tx = jnp.stack([first, 2 * EXONS_TX - first], axis=1).reshape(NTX)
    ends = jnp.cumsum(per_tx).astype(jnp.int32)
    exon_ids = jnp.arange(NEXON, dtype=jnp.int32)
    return jnp.sum((ends[None, :] <= exon_ids[:, None]).astype(jnp.int32), axis=1).astype(jnp.int32)


def draw_exon_transcript(key, part):
    return exon_owner(key)


def draw_exon_start(key, part):
    owner = exon_owner(key)
    offset = jax.random.randint(jax.random.fold_in(key, 12), (NEXON,), 0, SPAN).astype(jnp.int32)
    late = jax.random.randint(jax.random.fold_in(key, 13), (NEXON,), SPAN - 8, SPAN).astype(jnp.int32)
    next_owner = jnp.concatenate([owner[1:], jnp.full((1,), NTX, jnp.int32)])
    closing = next_owner != owner
    offset = jnp.where(closing, late, offset).astype(jnp.int32)
    start = jnp.minimum(owner * SPAN + offset, BINS - 32).astype(jnp.int32)
    start = start.at[0].set(0)
    start = start.at[NEXON - 1].set(BINS - 32)
    return start


def place_ends(entries, key, least, top_value):
    longest = entries.shape.index(max(entries.shape))
    spots = []
    for shift in (0, 1):
        where = [jax.random.randint(jax.random.fold_in(key, axis), (), 0, length) for axis, length in enumerate(entries.shape)]
        where[longest] = (where[longest] + shift) % entries.shape[longest]
        spots.append(tuple(where))
    return entries.at[spots[0]].set(least).at[spots[1]].set(top_value)


def shard_levels(own_key, extent, cuts, low, top_value):
    gain, own = 1.0, jax.random.fold_in(own_key, 6)
    for dim, blocks in cuts:
        draws = jnp.exp(jax.random.uniform(jax.random.fold_in(own, dim), (blocks,), jnp.float32, low / len(cuts), top_value / len(cuts)))
        gain = gain * jnp.repeat(draws, extent[dim] // blocks).reshape([-1 if axis == dim else 1 for axis in range(len(extent))])
    return gain


def bell_draw(key, shape, width, bound, split=(), kind=jnp.bfloat16):
    values = jax.random.normal(key, shape, jnp.float32) * width
    if len(split) > 0:
        values = shard_levels(key, shape, split, -0.22, 0.18) * values
    return jnp.clip(values, min=-bound, max=bound).astype(kind)


def setup_inputs(seed: int = 0) -> dict:
    key_of = jax.random.split(jax.random.key(seed), 13)
    stream = bell_draw(key_of[0], (BINS, CH), 1.0, 6.0, ((0, 8), (1, 4)))
    norm_gain = jnp.clip(1.0 + 0.15 * jax.random.normal(key_of[1], (LAYERS + 1, CH), jnp.float32), 0.25, 1.75)
    conv_weight = bell_draw(key_of[2], (LAYERS, 3, CH, HID), (3 * CH) ** -0.5, 0.09375, ((2, 8), (3, 4)))
    conv_bias = bell_draw(key_of[3], (LAYERS, HID), 0.5, 3.0, ((1, 4),), jnp.float32)
    point_weight = bell_draw(key_of[4], (LAYERS, HID, CH), HID ** -0.5, 0.21875, ((1, 8), (2, 4)))
    point_bias = bell_draw(key_of[5], (LAYERS, CH), 0.3, 2.0, ((1, 4),), jnp.float32)
    head_weight = bell_draw(key_of[6], (CH, TRACKS), CH ** -0.5, 0.15625, ((0, 8), (1, 4)))
    head_bias = bell_draw(key_of[7], (TRACKS,), 0.5, 3.0, ((0, 4),), jnp.float32)
    exon_start = draw_exon_start(jax.random.fold_in(key_of[12], 71), 0)
    exon_length = place_ends(jax.random.randint(key_of[9], (NEXON,), 1, 33), jax.random.fold_in(key_of[9], 1), 1, 32).astype(jnp.int32)
    exon_transcript = draw_exon_transcript(jax.random.fold_in(key_of[12], 71), 0)
    transcript_slot = jax.random.permutation(key_of[11], NTX).astype(jnp.int32)
    return dict(stream=stream, norm_gain=norm_gain, conv_weight=conv_weight, conv_bias=conv_bias, point_weight=point_weight, point_bias=point_bias, head_weight=head_weight, head_bias=head_bias, exon_start=exon_start, exon_length=exon_length, exon_transcript=exon_transcript, transcript_slot=transcript_slot)


def rms_scaled(values, gain_row):
    wide = values.astype(jnp.float32)
    scale = lax.rsqrt(lax.optimization_barrier(jnp.mean(wide * wide, axis=-1, keepdims=True)) + 1e-06)
    return wide * scale * gain_row

def reference(stream, norm_gain, conv_weight, conv_bias, point_weight, point_bias, head_weight, head_bias, exon_start, exon_length, exon_transcript, transcript_slot):
    resid = stream
    bin_count = stream.shape[0]
    for layer_idx in range(LAYERS):
        spread = 2 ** layer_idx
        act_rows = jax.nn.gelu(rms_scaled(resid, norm_gain[layer_idx]), approximate=False).astype(jnp.bfloat16)
        padded = jnp.pad(act_rows, ((spread, spread), (0, 0)))
        conv_sum = jnp.zeros((bin_count, conv_weight.shape[3]), jnp.float32)
        for tap_idx in range(3):
            conv_sum = conv_sum + jnp.dot(padded[tap_idx * spread:tap_idx * spread + bin_count], conv_weight[layer_idx, tap_idx], preferred_element_type=jnp.float32)
        hidden = jax.nn.gelu(conv_sum + conv_bias[layer_idx], approximate=False).astype(jnp.bfloat16)
        mixed = jnp.dot(hidden, point_weight[layer_idx], preferred_element_type=jnp.float32)
        resid = (resid.astype(jnp.float32) + mixed + point_bias[layer_idx]).astype(jnp.bfloat16)
    final_rows = rms_scaled(resid, norm_gain[LAYERS]).astype(jnp.bfloat16)
    coverage = jax.nn.softplus(jnp.dot(final_rows, head_weight, preferred_element_type=jnp.float32) + head_bias)
    bin_ids = jnp.arange(bin_count, dtype=jnp.int32)
    member = ((bin_ids[None, :] >= exon_start[:, None]) & (bin_ids[None, :] < (exon_start + exon_length)[:, None])).astype(jnp.bfloat16)
    owner_rows = transcript_slot[exon_transcript]
    select = (owner_rows[None, :] == jnp.arange(transcript_slot.shape[0], dtype=jnp.int32)[:, None]).astype(jnp.bfloat16)
    counts = jnp.dot(select, member, preferred_element_type=jnp.float32)
    total = jnp.dot(counts, coverage, precision=lax.Precision.HIGHEST)
    return jnp.log1p(total)
```

```python
import jax
import jax.numpy as jnp
from jax import lax
from jax.experimental import pallas as pl
from jax.experimental.pallas import tpu as pltpu
from jax.sharding import PartitionSpec as P

LAYERS = 8


def padded(block, sides, width):
    for axis, dim in sides:
        count = lax.axis_size(axis)
        forward = [(i, i + 1) for i in range(count - 1)]
        backward = [(target, source) for source, target in forward]
        low = lax.ppermute(
            lax.slice_in_dim(block, block.shape[dim] - width, None, axis=dim), axis, forward
        )
        high = lax.ppermute(lax.slice_in_dim(block, 0, width, axis=dim), axis, backward)
        block = jnp.concatenate([low, block, high], axis=dim)
    return block


def rms_scaled(values, gain_row):
    wide = values.astype(jnp.float32)
    scale = lax.rsqrt(jnp.mean(wide * wide, axis=-1, keepdims=True) + 1e-06)
    return wide * scale * gain_row


def local_plain(
    stream,
    norm_gain,
    conv_weight,
    conv_bias,
    point_weight,
    point_bias,
    head_weight,
    head_bias,
    exon_start,
    exon_length,
    exon_transcript,
    transcript_slot,
):
    bin_rows = stream.shape[0]
    resid = stream
    for layer_idx in range(LAYERS):
        spread = 2**layer_idx
        rimmed = padded(resid, (("seq", 0),), spread)
        full_rows = lax.all_gather(rimmed, "ch", axis=1, tiled=True)
        act_rows = jax.nn.gelu(
            rms_scaled(full_rows, norm_gain[layer_idx]), approximate=False
        ).astype(jnp.bfloat16)
        tap_rows = jnp.stack(
            [
                act_rows[0:bin_rows],
                act_rows[spread : spread + bin_rows],
                act_rows[2 * spread : 2 * spread + bin_rows],
            ]
        )
        conv_sum = jnp.einsum(
            "kbc,kch->bh",
            tap_rows,
            lax.all_gather(conv_weight[layer_idx], "seq", axis=1, tiled=True),
            preferred_element_type=jnp.float32,
        )
        hidden = jax.nn.gelu(conv_sum + conv_bias[layer_idx], approximate=False).astype(
            jnp.bfloat16
        )
        hidden_all = lax.all_gather(hidden, "ch", axis=1, tiled=True)
        mixed = jnp.dot(
            hidden_all,
            lax.all_gather(point_weight[layer_idx], "seq", axis=0, tiled=True),
            preferred_element_type=jnp.float32,
        )
        resid = (resid.astype(jnp.float32) + mixed + point_bias[layer_idx]).astype(jnp.bfloat16)
    final_all = lax.all_gather(resid, "ch", axis=1, tiled=True)
    final_rows = rms_scaled(final_all, norm_gain[LAYERS]).astype(jnp.bfloat16)
    logits = jnp.dot(
        final_rows,
        lax.all_gather(head_weight, "seq", axis=0, tiled=True),
        preferred_element_type=jnp.float32,
    )
    coverage = jax.nn.softplus(logits + head_bias)
    seq_index = lax.axis_index("seq")
    bin_ids = seq_index * bin_rows + jnp.arange(bin_rows, dtype=jnp.int32)
    member = (
        (bin_ids[None, :] >= exon_start[:, None])
        & (bin_ids[None, :] < (exon_start + exon_length)[:, None])
    ).astype(jnp.bfloat16)
    owner_rows = transcript_slot[exon_transcript]
    select = (
        owner_rows[None, :] == jnp.arange(transcript_slot.shape[0], dtype=jnp.int32)[:, None]
    ).astype(jnp.bfloat16)
    counts = jnp.dot(select, member, preferred_element_type=jnp.float32)
    total = lax.psum_scatter(
        jnp.dot(counts, coverage, precision=lax.Precision.HIGHEST),
        "seq",
        scatter_dimension=0,
        tiled=True,
    )
    return jnp.log1p(total)


SEQ = 8
CHS = 4
BOTH = 0
START = 2
TILE = 32
CHUNKS = 960 // TILE
GROUP = 64
GROUPS = 960 // GROUP
IDLE = 3
EARLY = 192 // TILE
STEP = 448
CONV = 640
KEPT = 384
WIDE = 256
HEADW = 1024
MESH = pl.DeviceIdType.MESH
OFFSETS = (0, 1, -1, 2, -2, 3, -3, 4)


def gelu(values):
    return 0.5 * values * (1.0 + lax.erf(values * 0.7071067811865476))


def at_place(spot):
    spot = (spot + 2 * SEQ) % SEQ
    upper = spot // (SEQ // 2)
    return (1 - upper) * 2 * spot + upper * (2 * (SEQ - 1 - spot) + 1)


def tower_kernel(
    x_ref,
    gain_ref,
    conv_ref,
    conv_bias_ref,
    point_ref,
    point_bias_ref,
    head_ref,
    head_bias_ref,
    start_ref,
    length_ref,
    owner_ref,
    slot_ref,
    out_ref,
    pack_conv,
    pack_head,
    conv_w,
    point_w,
    head_w,
    small,
    inbox,
    outbox,
    past,
    past_x,
    act,
    hid,
    counts,
    conv_bias,
    point_bias,
    head_bias,
    finals,
    total,
    landed,
    w_send,
    w_recv,
    f_send,
    h_send,
    h_recv,
    g_send,
    g_recv,
    s_send,
    s_recv,
    x_send,
    x_recv,
    c_send,
    t_send,
    t_recv,
):
    seq = lax.axis_index("seq")
    ch = lax.axis_index("ch")
    odd = seq % 2
    place = (1 - odd) * (seq // 2) + odd * (SEQ - 1 - seq // 2)
    stage = (place - START + SEQ) % SEQ
    sibling = ch + 1 - 2 * (ch % 2)
    across = (ch + 2) % CHS
    diagonal = (sibling + 2) % CHS
    first_seq = at_place(START)
    rows, width = x_ref.shape
    chans = width * CHS
    depth = conv_ref.shape[2]
    lines = point_ref.shape[1]

    barrier = pltpu.get_barrier_semaphore()

    @pl.loop(1, SEQ * CHS)
    def _(step):
        peer = (seq * CHS + ch + step) % (SEQ * CHS)
        pl.semaphore_signal(
            barrier, inc=1, device_id=(peer // CHS, peer % CHS), device_id_type=MESH
        )

    def remote(src, dst, send, recv, target):
        return pltpu.make_async_remote_copy(
            src_ref=src,
            dst_ref=dst,
            send_sem=send,
            recv_sem=recv,
            device_id=target,
            device_id_type=MESH,
        )

    def conv_spot(origin, block):
        return conv_w.at[
            pl.ds(pl.multiple_of(origin * depth, 64), depth),
            pl.ds(pl.multiple_of(block * CONV, 128), CONV),
        ]

    def point_spot(origin, block):
        row = (origin // 2) * WIDE + (origin % 2) * lines
        return point_w.at[
            pl.ds(pl.multiple_of(row, 32), lines),
            pl.ds(pl.multiple_of(block * width, 128), width),
        ]

    def head_spot(origin):
        return head_w.at[pl.ds(pl.multiple_of(origin * depth, 64), depth)]

    def pack(layer):
        taps = [conv_ref[layer, tap] for tap in range(3)]
        own = pack_conv.at[layer]
        own[:, 0:128] = taps[0][:, 0:128]
        own[:, 128:256] = taps[1][:, 0:128]
        own[:, 256:384] = jnp.concatenate([taps[0][:, 128:192], taps[1][:, 128:192]], axis=1)
        own[:, 384:512] = taps[2][:, 0:128]
        own[:, 512:640] = jnp.concatenate(
            [taps[2][:, 128:192], jnp.zeros((depth, 64), jnp.bfloat16)], axis=1
        )

    def layer_copies(layer, peer, number):
        target = (at_place(layer + START), peer)
        return (
            remote(
                pack_conv.at[layer],
                conv_spot(seq, ch),
                w_send.at[number, layer, 0],
                w_recv.at[number, seq, 0],
                target,
            ),
            remote(
                point_ref.at[layer],
                point_spot(seq, ch),
                w_send.at[number, layer, 1],
                w_recv.at[number, seq, 1],
                target,
            ),
        )

    def own_layer():
        return (
            pltpu.make_async_copy(
                pack_conv.at[stage], conv_spot(seq, ch), w_recv.at[0, seq, 0]
            ),
            pltpu.make_async_copy(
                point_ref.at[stage], point_spot(seq, ch), w_recv.at[0, seq, 1]
            ),
        )

    def each_layer(act_on):
        for offset in OFFSETS[1:]:
            layer = (stage + offset + SEQ) % SEQ
            act_on(layer, layer_copies(layer, ch, 0))

            @pl.when(layer < BOTH)
            def _():
                act_on(None, layer_copies(layer, across, 1))

    def start_layer(layer, copies):
        if layer is not None:
            pack(layer)
        for copy in copies:
            copy.start()

    def finish_layer(layer, copies):
        for copy in copies:
            copy.wait_send()

    def head_copy():
        return remote(pack_head, head_spot(seq), h_send, h_recv.at[seq], (first_seq, ch))

    def own_head():
        return pltpu.make_async_copy(pack_head, head_spot(seq), h_recv.at[seq])

    def stream_sends(act_on):
        parts = rows // TILE
        for dest in range(CHS):
            for part in range(parts):
                chunk = seq * parts + part - (STEP // TILE) * dest
                inside = (chunk >= 0) & (chunk < CHUNKS)
                chunk_at = jnp.clip(chunk, 0, CHUNKS - 1)
                mine = (seq == first_seq) & (ch == dest)
                src = x_ref.at[pl.ds(part * TILE, TILE)]
                dst = inbox.at[
                    chunk_at, :, pl.ds(pl.multiple_of(ch * width, 128), width)
                ]
                act_on(dest, part, inside, mine, chunk_at, src, dst)

    def start_early(dest, part, inside, *rest):
        start_stream(dest, part, inside & (rest[1] < EARLY), *rest)

    def start_late(dest, part, inside, *rest):
        start_stream(dest, part, inside & (rest[1] >= EARLY), *rest)

    def start_stream(dest, part, inside, mine, chunk, src, dst):
        @pl.when(inside & mine)
        def _():
            pltpu.make_async_copy(src, dst, x_recv.at[chunk]).start()

        @pl.when(inside & jnp.logical_not(mine))
        def _():
            remote(
                src, dst, c_send.at[dest, part], x_recv.at[chunk], (first_seq, dest)
            ).start()

    def finish_stream(dest, part, inside, mine, chunk, src, dst):
        @pl.when(inside & jnp.logical_not(mine))
        def _():
            remote(
                src, dst, c_send.at[dest, part], x_recv.at[chunk], (first_seq, dest)
            ).wait_send()

    pack(stage)
    own_small = small.at[ch]
    own_small[...] = jnp.zeros(own_small.shape, jnp.float32)
    own_small[0:LAYERS, 0 : conv_bias_ref.shape[1]] = conv_bias_ref[...]
    own_small[0:LAYERS, WIDE : WIDE + width] = point_bias_ref[...]
    head_bias[...] = jnp.zeros_like(head_bias)
    head_bias[:, 0 : head_bias_ref.shape[1]] = head_bias_ref[...]
    used = 2 * lines
    for block in range(CHS):
        point_w[block * WIDE + used : (block + 1) * WIDE, :] = jnp.zeros(
            (WIDE - used, chans), jnp.bfloat16
        )
    pl.semaphore_wait(barrier, SEQ * CHS - 1)

    for copy in own_layer():
        copy.start()
    small_copies = [
        remote(
            small.at[ch], small.at[ch], s_send.at[number], s_recv.at[number], (seq, peer)
        )
        for number, peer in enumerate((across, sibling, diagonal))
    ]
    for copy in small_copies:
        copy.start()
    stream_sends(start_early)
    each_layer(start_layer)
    tracks = head_ref.shape[1]
    edge = tracks // 128 * 128
    pack_head[:, edge:] = jnp.zeros((depth, HEADW - edge), jnp.bfloat16)
    pack_head[:, 0:tracks] = head_ref[...]

    @pl.when(seq == first_seq)
    def _():
        own_head().start()

    @pl.when(seq != first_seq)
    def _():
        head_copy().start()

    past[0:256, :] = jnp.zeros((256, past.shape[1]), jnp.float32)
    past_x[0:128, :] = jnp.zeros((128, chans), jnp.float32)

    @pl.when(seq == first_seq)
    def _():
        slots = slot_ref.shape[1]

        @pl.when(ch == CHS - 1)
        def _():
            for chunk in range((SEQ * rows - STEP * (CHS - 1)) // TILE, CHUNKS):
                inbox[chunk] = jnp.zeros((TILE, chans), jnp.bfloat16)

        @pl.loop(0, GROUPS - IDLE)
        def _(group):
            place_in = lax.broadcasted_iota(
                jnp.int32, (CHS * GROUP, start_ref.shape[1]), 0
            )
            quarter = place_in // GROUP
            local_row = (group + IDLE) * GROUP + place_in % GROUP
            bins = quarter * STEP + local_row - (2**LAYERS - 1)
            least = 255 + 256 * jnp.minimum(quarter, 1)
            owned_bin = (local_row >= least) & (local_row < GROUPS * GROUP - 1)
            member = (
                (bins >= start_ref[...])
                & (bins < start_ref[...] + length_ref[...])
                & owned_bin
            )
            names = lax.broadcasted_iota(jnp.int32, (slots, owner_ref.shape[1]), 0)
            owned = lax.dot_general(
                jnp.where(names == owner_ref[...], 1.0, 0.0).astype(jnp.bfloat16),
                jnp.where(member, 1.0, 0.0).astype(jnp.bfloat16),
                (((1,), (1,)), ((), ())),
                preferred_element_type=jnp.float32,
            )
            order = lax.broadcasted_iota(jnp.int32, (slots, slots), 0) == slot_ref[...]
            counts[group] = jnp.dot(
                jnp.where(order, 1.0, 0.0).astype(jnp.bfloat16),
                owned.astype(jnp.bfloat16),
                preferred_element_type=jnp.float32,
            ).astype(jnp.bfloat16)

    def arrive(number, origin):
        block = (ch, across, sibling, diagonal)[number]
        for part, spot in ((0, conv_spot(origin, block)), (1, point_spot(origin, block))):
            remote(
                spot, spot, f_send.at[0, 0, 0], w_recv.at[number, origin, part], (seq, sibling)
            ).wait_recv()

    def forward(number, origin, kind):
        block = (ch, across)[number]
        peer, arrival = ((across, 1), (sibling, 2), (sibling, 3))[kind]
        return [
            remote(
                spot,
                spot,
                f_send.at[kind, origin, part],
                w_recv.at[arrival, origin, part],
                (seq, peer),
            )
            for part, spot in (
                (0, conv_spot(origin, block)),
                (1, point_spot(origin, block)),
            )
        ]

    def across_too(origin):
        return (stage >= BOTH) | (origin == seq)

    def take_direct(origin):
        arrive(0, origin)

        @pl.when(across_too(origin))
        def _():
            for copy in forward(0, origin, 0):
                copy.start()

        for copy in forward(0, origin, 1):
            copy.start()

    def take_across(origin):
        arrive(1, origin)
        for copy in forward(1, origin, 2):
            copy.start()

    origins = [at_place(place + offset) for offset in OFFSETS]
    for number, origin in enumerate(origins):
        take_direct(origin)
        if number:
            take_across(origins[number - 1])
    take_across(origins[-1])
    for copy in small_copies:
        copy.wait_recv()
    for block in range(CHS):
        conv_bias[:, block * WIDE : (block + 1) * WIDE] = small[block, pl.ds(stage, 1), 0:WIDE]
        point_bias[:, block * width : (block + 1) * width] = small[
            block, pl.ds(stage, 1), WIDE : WIDE + width
        ]
    for origin in origins:
        arrive(2, origin)
        arrive(3, origin)
    stream_sends(start_late)


    spread = 1
    for number in range(1, SEQ):
        spread = spread + (2 ** (number - 1)) * jnp.where(stage >= number, 1, 0)
    after = at_place(place + 1)

    def norm_rows(slot, turn, first, count):
        wide = inbox[slot, pl.ds(first, count), :].astype(jnp.float32)
        squares = jnp.sum(wide * wide, axis=1, keepdims=True)
        scale = lax.rsqrt(squares / chans + 1e-06)
        return wide, wide * scale * gain_ref[pl.ds(turn, 1), :]

    def hop(chunk):
        landing = chunk + CHUNKS * jnp.where(stage == SEQ - 1, 1, 0)
        return remote(
            outbox.at[chunk], inbox.at[landing], x_send.at[chunk], x_recv.at[landing], (after, ch)
        )

    def inbox_arrive(slot):
        remote(
            inbox.at[slot], inbox.at[slot], x_send.at[0], x_recv.at[slot], (after, ch)
        ).wait_recv()

    sub = 16

    def shifted(ref, base, lag, lanes):
        steps = (lag + 7) // 8
        window = ref[pl.ds(pl.multiple_of(base - steps * 8, 8), TILE + 8), lanes]
        turn = (TILE + 8 - steps * 8 + lag) % (TILE + 8)
        return pltpu.roll(window, turn, 0)[0:TILE]

    def run_chunk(chunk):
        base = pl.multiple_of(chunk * TILE, TILE)

        absent = (seq == first_seq) & (
            ch * STEP + chunk * TILE >= SEQ * rows
        )

        @pl.when(jnp.logical_not(absent))
        def _():
            inbox_arrive(chunk)

        for first in range(0, TILE, sub):
            wide, normed = norm_rows(chunk, stage, first, sub)
            bins = (
                ch * STEP
                + chunk * TILE
                + first
                - (spread - 1)
                + lax.broadcasted_iota(jnp.int32, (sub, chans), 0)
            )
            inside = (bins >= 0) & (bins < SEQ * rows)
            act[first : first + sub, :] = jnp.where(inside, gelu(normed), 0.0).astype(
                jnp.bfloat16
            )
            past_x[pl.ds(128 + base + first, sub), :] = wide
        for block in range(CHS):
            taps = jnp.dot(
                act[...],
                conv_w[:, block * CONV : (block + 1) * CONV],
                preferred_element_type=jnp.float32,
            )
            lane = block * KEPT
            past[pl.ds(256 + base, TILE), lane : lane + KEPT] = taps[:, 0:KEPT]
            far, near = 2 * spread, spread
            left = (
                shifted(past, 256 + base, far, slice(lane, lane + 128))
                + shifted(past, 256 + base, near, slice(lane + 128, lane + 256))
                + taps[:, KEPT : KEPT + 128]
                + conv_bias[:, block * WIDE : block * WIDE + 128]
            )
            right = (
                shifted(past, 256 + base, far, slice(lane + 256, lane + 384))
                + pltpu.roll(shifted(past, 256 + base, near, slice(lane + 256, lane + 384)), 64, 1)
                + taps[:, KEPT + 128 : CONV]
                + conv_bias[:, block * WIDE + 128 : (block + 1) * WIDE]
            )
            hid[:, block * WIDE : block * WIDE + 128] = gelu(left).astype(jnp.bfloat16)
            hid[:, block * WIDE + 128 : (block + 1) * WIDE] = gelu(right).astype(jnp.bfloat16)
        for block in range(CHS):
            lanes = slice(block * width, (block + 1) * width)
            mixed = jnp.dot(hid[...], point_w[:, lanes], preferred_element_type=jnp.float32)
            outbox[chunk, :, lanes] = (
                shifted(past_x, 128 + base, spread, lanes) + mixed + point_bias[:, lanes]
            ).astype(jnp.bfloat16)
        hop(chunk).start()

    @pl.loop(0, CHUNKS)
    def _(chunk):
        run_chunk(chunk)

    def total_copy(origin):
        return remote(
            total.at[pl.ds(origin * 8, 8)],
            landed,
            t_send.at[origin],
            t_recv,
            (origin, ch),
        )

    def final_copies(group):
        def copy(block, peer, number):
            return remote(
                finals.at[group, block],
                finals.at[group, block],
                g_send.at[number, group],
                g_recv.at[number, group],
                (seq, peer),
            )

        return copy(ch, across, 0), copy(ch, sibling, 1), copy(across, sibling, 2)

    def give_group(group):
        for part in range(GROUP // TILE):
            slot = CHUNKS + (group + IDLE) * (GROUP // TILE) + part
            inbox_arrive(slot)
            for first in range(0, TILE, sub):
                _, normed = norm_rows(slot, LAYERS, first, sub)
                start = part * TILE + first
                finals[group, ch, start : start + sub, :] = normed.astype(jnp.bfloat16)
        to_across, to_sibling, _ = final_copies(group)
        to_across.start()
        to_sibling.start()

    def take_group(group):
        to_across, to_sibling, onward = final_copies(group)
        to_across.wait_recv()
        onward.start()
        to_sibling.wait_recv()
        onward.wait_recv()
        rows_in = finals[group].reshape(CHS * GROUP, chans)
        for start in range(0, HEADW, 256):
            lanes = slice(start, start + 256)
            logits = (
                jnp.dot(rows_in, head_w[:, lanes], preferred_element_type=jnp.float32)
                + head_bias[:, lanes]
            )
            cover = jnp.maximum(logits, 0.0) + jnp.log1p(jnp.exp(-jnp.abs(logits)))
            sums = total[:, lanes]
            for _ in range(3):
                piece = cover.astype(jnp.bfloat16)
                sums = sums + jnp.dot(
                    counts[group], piece, preferred_element_type=jnp.float32
                )
                cover = cover - piece.astype(jnp.float32)
            total[:, lanes] = sums

    @pl.when(seq == first_seq)
    def _():
        for origin in origins:
            head_copy_in = remote(
                pack_head, head_spot(origin), h_send, h_recv.at[origin], (seq, sibling)
            )
            head_copy_in.wait_recv()
        total[...] = jnp.zeros_like(total)

        @pl.loop(0, IDLE * GROUP // TILE)
        def _(chunk):
            inbox_arrive(CHUNKS + chunk)

        give_group(0)

        @pl.loop(1, GROUPS - IDLE)
        def _(group):
            give_group(group)
            take_group(group - 1)

        take_group(GROUPS - IDLE - 1)
        for origin in range(SEQ):

            @pl.when(origin == first_seq)
            def _():
                pltpu.make_async_copy(total.at[pl.ds(origin * 8, 8)], landed, t_recv).start()

            @pl.when(origin != first_seq)
            def _():
                total_copy(origin).start()

    each_layer(finish_layer)

    @pl.when(seq != first_seq)
    def _():
        head_copy().wait_send()

    stream_sends(finish_stream)
    for copy in small_copies:
        copy.wait_send()
    for origin in origins:

        @pl.when(across_too(origin))
        def _():
            for copy in forward(0, origin, 0):
                copy.wait_send()

        for copy in forward(0, origin, 1) + forward(1, origin, 2):
            copy.wait_send()

    @pl.loop(0, CHUNKS)
    def _(chunk):
        hop(chunk).wait_send()

    remote(landed, landed, t_send.at[0], t_recv, (seq, sibling)).wait_recv()
    out_ref[...] = jnp.log1p(landed[...])[:, : out_ref.shape[1]]

    @pl.when(seq == first_seq)
    def _():
        @pl.loop(0, GROUPS - IDLE)
        def _(group):
            for copy in final_copies(group):
                copy.wait_send()

        for origin in range(SEQ):

            @pl.when(origin != first_seq)
            def _():
                total_copy(origin).wait_send()


def local_kernel(
    stream,
    norm_gain,
    conv_weight,
    conv_bias,
    point_weight,
    point_bias,
    head_weight,
    head_bias,
    exon_start,
    exon_length,
    exon_transcript,
    transcript_slot,
):
    rows, width = stream.shape
    depth = conv_weight.shape[2]
    tracks = head_weight.shape[1]
    slots = transcript_slot.shape[0]
    chans = CHS * width
    vmem = pl.BlockSpec(memory_space=pltpu.VMEM)
    dma = pltpu.SemaphoreType.DMA
    f32, bf16 = jnp.float32, jnp.bfloat16
    return pl.pallas_call(
        tower_kernel,
        out_shape=jax.ShapeDtypeStruct((slots // SEQ, tracks), f32),
        in_specs=[vmem] * 12,
        out_specs=vmem,
        scratch_shapes=[
            pltpu.VMEM((LAYERS, depth, CONV), bf16),
            pltpu.VMEM((depth, HEADW), bf16),
            pltpu.VMEM((chans, CHS * CONV), bf16),
            pltpu.VMEM((CHS * WIDE, chans), bf16),
            pltpu.VMEM((chans, HEADW), bf16),
            pltpu.VMEM((CHS, 8, 640), f32),
            pltpu.VMEM((2 * CHUNKS, TILE, chans), bf16),
            pltpu.VMEM((CHUNKS, TILE, chans), bf16),
            pltpu.VMEM((264 + CHUNKS * TILE, CHS * KEPT), f32),
            pltpu.VMEM((136 + CHUNKS * TILE, chans), f32),
            pltpu.VMEM((TILE, chans), bf16),
            pltpu.VMEM((TILE, CHS * WIDE), bf16),
            pltpu.VMEM((GROUPS - IDLE, slots, CHS * GROUP), bf16),
            pltpu.VMEM((1, CHS * WIDE), f32),
            pltpu.VMEM((1, chans), f32),
            pltpu.VMEM((1, HEADW), f32),
            pltpu.VMEM((GROUPS - IDLE, CHS, GROUP, chans), bf16),
            pltpu.VMEM((slots, HEADW), f32),
            pltpu.VMEM((slots // SEQ, HEADW), f32),
            dma((2, LAYERS, 2)),
            dma((4, SEQ, 2)),
            dma((3, SEQ, 2)),
            dma(()),
            dma((SEQ,)),
            dma((3, GROUPS - IDLE)),
            dma((3, GROUPS - IDLE)),
            dma((3,)),
            dma((3,)),
            dma((CHUNKS,)),
            dma((2 * CHUNKS,)),
            dma((CHS, rows // TILE)),
            dma((SEQ,)),
            dma(()),
        ],
        compiler_params=pltpu.CompilerParams(
            collective_id=0, has_side_effects=True, vmem_limit_bytes=60 * 2**20
        ),
        cost_estimate=pl.CostEstimate(
            flops=20_000_000_000, bytes_accessed=4_000_000, transcendentals=8_000_000
        ),
    )(
        stream,
        norm_gain,
        conv_weight,
        conv_bias,
        point_weight,
        point_bias,
        head_weight,
        head_bias[None, :],
        exon_start[None, :],
        exon_length[None, :],
        exon_transcript[None, :],
        transcript_slot[None, :],
    )


def local(*args):
    stream, conv_weight, point_weight, head_weight = args[0], args[2], args[4], args[6]
    fits = (
        lax.axis_size("seq") == SEQ
        and lax.axis_size("ch") == CHS
        and stream.shape == (256, 384)
        and conv_weight.shape[1:] == (3, 192, 192)
        and point_weight.shape[1:] == (96, 384)
        and head_weight.shape == (192, 960)
        and args[11].shape[0] == 8 * SEQ
    )
    return local_kernel(*args) if fits else local_plain(*args)


def solution(mesh):
    placed = (
        P("seq", "ch"),
        P(),
        P(None, None, "seq", "ch"),
        P(None, "ch"),
        P(None, "seq", "ch"),
        P(None, "ch"),
        P("seq", "ch"),
        P("ch"),
        P(),
        P(),
        P(),
        P(),
    )
    return jax.shard_map(
        local, mesh=mesh, in_specs=placed, out_specs=P("seq", "ch"), check_vma=False
    )
```

```python
import jax
import jax.numpy as jnp
from jax import lax
from jax.experimental import pallas as pl
from jax.experimental.pallas import tpu as pltpu
from jax.sharding import PartitionSpec as P

LAYERS = 8


def padded(block, sides, width):
    for axis, dim in sides:
        count = lax.axis_size(axis)
        forward = [(i, i + 1) for i in range(count - 1)]
        backward = [(target, source) for source, target in forward]
        low = lax.ppermute(
            lax.slice_in_dim(block, block.shape[dim] - width, None, axis=dim), axis, forward
        )
        high = lax.ppermute(lax.slice_in_dim(block, 0, width, axis=dim), axis, backward)
        block = jnp.concatenate([low, block, high], axis=dim)
    return block


def rms_scaled(values, gain_row):
    wide = values.astype(jnp.float32)
    scale = lax.rsqrt(jnp.mean(wide * wide, axis=-1, keepdims=True) + 1e-06)
    return wide * scale * gain_row


def local_plain(
    stream,
    norm_gain,
    conv_weight,
    conv_bias,
    point_weight,
    point_bias,
    head_weight,
    head_bias,
    exon_start,
    exon_length,
    exon_transcript,
    transcript_slot,
):
    bin_rows = stream.shape[0]
    resid = stream
    for layer_idx in range(LAYERS):
        spread = 2**layer_idx
        rimmed = padded(resid, (("seq", 0),), spread)
        full_rows = lax.all_gather(rimmed, "ch", axis=1, tiled=True)
        act_rows = jax.nn.gelu(
            rms_scaled(full_rows, norm_gain[layer_idx]), approximate=False
        ).astype(jnp.bfloat16)
        tap_rows = jnp.stack(
            [
                act_rows[0:bin_rows],
                act_rows[spread : spread + bin_rows],
                act_rows[2 * spread : 2 * spread + bin_rows],
            ]
        )
        conv_sum = jnp.einsum(
            "kbc,kch->bh",
            tap_rows,
            lax.all_gather(conv_weight[layer_idx], "seq", axis=1, tiled=True),
            preferred_element_type=jnp.float32,
        )
        hidden = jax.nn.gelu(conv_sum + conv_bias[layer_idx], approximate=False).astype(
            jnp.bfloat16
        )
        hidden_all = lax.all_gather(hidden, "ch", axis=1, tiled=True)
        mixed = jnp.dot(
            hidden_all,
            lax.all_gather(point_weight[layer_idx], "seq", axis=0, tiled=True),
            preferred_element_type=jnp.float32,
        )
        resid = (resid.astype(jnp.float32) + mixed + point_bias[layer_idx]).astype(jnp.bfloat16)
    final_all = lax.all_gather(resid, "ch", axis=1, tiled=True)
    final_rows = rms_scaled(final_all, norm_gain[LAYERS]).astype(jnp.bfloat16)
    logits = jnp.dot(
        final_rows,
        lax.all_gather(head_weight, "seq", axis=0, tiled=True),
        preferred_element_type=jnp.float32,
    )
    coverage = jax.nn.softplus(logits + head_bias)
    seq_index = lax.axis_index("seq")
    bin_ids = seq_index * bin_rows + jnp.arange(bin_rows, dtype=jnp.int32)
    member = (
        (bin_ids[None, :] >= exon_start[:, None])
        & (bin_ids[None, :] < (exon_start + exon_length)[:, None])
    ).astype(jnp.bfloat16)
    owner_rows = transcript_slot[exon_transcript]
    select = (
        owner_rows[None, :] == jnp.arange(transcript_slot.shape[0], dtype=jnp.int32)[:, None]
    ).astype(jnp.bfloat16)
    counts = jnp.dot(select, member, preferred_element_type=jnp.float32)
    total = lax.psum_scatter(
        jnp.dot(counts, coverage, precision=lax.Precision.HIGHEST),
        "seq",
        scatter_dimension=0,
        tiled=True,
    )
    return jnp.log1p(total)


SEQ = 8
CHS = 4
BOTH = 0
START = 2
TILE = 32
CHUNKS = 960 // TILE
GROUP = 96
GROUPS = 960 // GROUP
IDLE = 2
EARLY = 192 // TILE
STEP = 448
CONV = 640
KEPT = 384
WIDE = 256
HEADW = 1024
MESH = pl.DeviceIdType.MESH
OFFSETS = (0, 1, -1, 2, -2, 3, -3, 4)


def gelu(values):
    return 0.5 * values * (1.0 + lax.erf(values * 0.7071067811865476))


def at_place(spot):
    spot = (spot + 2 * SEQ) % SEQ
    upper = spot // (SEQ // 2)
    return (1 - upper) * 2 * spot + upper * (2 * (SEQ - 1 - spot) + 1)


def tower_kernel(
    x_ref,
    gain_ref,
    conv_ref,
    conv_bias_ref,
    point_ref,
    point_bias_ref,
    head_ref,
    head_bias_ref,
    start_ref,
    length_ref,
    owner_ref,
    slot_ref,
    out_ref,
    pack_conv,
    pack_head,
    conv_w,
    point_w,
    head_w,
    small,
    inbox,
    outbox,
    past,
    past_x,
    act,
    hid,
    counts,
    conv_bias,
    point_bias,
    head_bias,
    finals,
    total,
    landed,
    w_send,
    w_recv,
    f_send,
    h_send,
    h_recv,
    g_send,
    g_recv,
    s_send,
    s_recv,
    x_send,
    x_recv,
    c_send,
    e_send,
    t_send,
    t_recv,
):
    seq = lax.axis_index("seq")
    ch = lax.axis_index("ch")
    odd = seq % 2
    place = (1 - odd) * (seq // 2) + odd * (SEQ - 1 - seq // 2)
    stage = (place - START + SEQ) % SEQ
    sibling = ch + 1 - 2 * (ch % 2)
    across = (ch + 2) % CHS
    diagonal = (sibling + 2) % CHS
    first_seq = at_place(START)
    rows, width = x_ref.shape
    chans = width * CHS
    depth = conv_ref.shape[2]
    lines = point_ref.shape[1]

    barrier = pltpu.get_barrier_semaphore()

    @pl.loop(1, SEQ * CHS)
    def _(step):
        peer = (seq * CHS + ch + step) % (SEQ * CHS)
        pl.semaphore_signal(
            barrier, inc=1, device_id=(peer // CHS, peer % CHS), device_id_type=MESH
        )

    def remote(src, dst, send, recv, target):
        return pltpu.make_async_remote_copy(
            src_ref=src,
            dst_ref=dst,
            send_sem=send,
            recv_sem=recv,
            device_id=target,
            device_id_type=MESH,
        )

    def conv_spot(origin, block):
        return conv_w.at[
            pl.ds(pl.multiple_of(origin * depth, 64), depth),
            pl.ds(pl.multiple_of(block * CONV, 128), CONV),
        ]

    def point_spot(origin, block):
        row = (origin // 2) * WIDE + (origin % 2) * lines
        return point_w.at[
            pl.ds(pl.multiple_of(row, 32), lines),
            pl.ds(pl.multiple_of(block * width, 128), width),
        ]

    def head_spot(origin):
        return head_w.at[pl.ds(pl.multiple_of(origin * depth, 64), depth)]

    def pack(layer):
        taps = [conv_ref[layer, tap] for tap in range(3)]
        own = pack_conv.at[layer]
        own[:, 0:128] = taps[0][:, 0:128]
        own[:, 128:256] = taps[1][:, 0:128]
        own[:, 256:384] = jnp.concatenate([taps[0][:, 128:192], taps[1][:, 128:192]], axis=1)
        own[:, 384:512] = taps[2][:, 0:128]
        own[:, 512:640] = jnp.concatenate(
            [taps[2][:, 128:192], jnp.zeros((depth, 64), jnp.bfloat16)], axis=1
        )

    def layer_copies(layer, peer, number):
        target = (at_place(layer + START), peer)
        return (
            remote(
                pack_conv.at[layer],
                conv_spot(seq, ch),
                w_send.at[number, layer, 0],
                w_recv.at[number, seq, 0],
                target,
            ),
            remote(
                point_ref.at[layer],
                point_spot(seq, ch),
                w_send.at[number, layer, 1],
                w_recv.at[number, seq, 1],
                target,
            ),
        )

    def own_layer():
        return (
            pltpu.make_async_copy(
                pack_conv.at[stage], conv_spot(seq, ch), w_recv.at[0, seq, 0]
            ),
            pltpu.make_async_copy(
                point_ref.at[stage], point_spot(seq, ch), w_recv.at[0, seq, 1]
            ),
        )

    def each_layer(act_on):
        for offset in OFFSETS[1:]:
            layer = (stage + offset + SEQ) % SEQ
            act_on(layer, layer_copies(layer, ch, 0))

            @pl.when(layer < BOTH)
            def _():
                act_on(None, layer_copies(layer, across, 1))

    def start_layer(layer, copies):
        if layer is not None:
            pack(layer)
        for copy in copies:
            copy.start()

    def finish_layer(layer, copies):
        for copy in copies:
            copy.wait_send()

    def head_copy():
        return remote(pack_head, head_spot(seq), h_send, h_recv.at[seq], (first_seq, ch))

    def own_head():
        return pltpu.make_async_copy(pack_head, head_spot(seq), h_recv.at[seq])

    def stream_sends(act_on):
        parts = rows // TILE
        for dest in range(CHS):
            for part in range(parts):
                chunk = seq * parts + part - (STEP // TILE) * dest
                inside = (chunk >= 0) & (chunk < (CHUNKS if dest % 2 else STEP // TILE))
                chunk_at = jnp.clip(chunk, 0, CHUNKS - 1)
                mine = (seq == first_seq) & (ch == dest)
                src = x_ref.at[pl.ds(part * TILE, TILE)]
                dst = inbox.at[
                    chunk_at, :, pl.ds(pl.multiple_of(ch * width, 128), width)
                ]
                act_on(dest, part, inside, mine, chunk_at, src, dst)

    def start_early(dest, part, inside, *rest):
        start_stream(dest, part, inside & (rest[1] < EARLY), *rest)

    def start_late(dest, part, inside, *rest):
        start_stream(dest, part, inside & (rest[1] >= EARLY), *rest)

    def start_stream(dest, part, inside, mine, chunk, src, dst):
        @pl.when(inside & mine)
        def _():
            pltpu.make_async_copy(src, dst, x_recv.at[chunk]).start()

        @pl.when(inside & jnp.logical_not(mine))
        def _():
            remote(
                src, dst, c_send.at[dest, part], x_recv.at[chunk], (first_seq, dest)
            ).start()

    def finish_stream(dest, part, inside, mine, chunk, src, dst):
        @pl.when(inside & jnp.logical_not(mine))
        def _():
            remote(
                src, dst, c_send.at[dest, part], x_recv.at[chunk], (first_seq, dest)
            ).wait_send()

    pack(stage)
    own_small = small.at[ch]
    own_small[...] = jnp.zeros(own_small.shape, jnp.float32)
    own_small[0:LAYERS, 0 : conv_bias_ref.shape[1]] = conv_bias_ref[...]
    own_small[0:LAYERS, WIDE : WIDE + width] = point_bias_ref[...]
    head_bias[...] = jnp.zeros_like(head_bias)
    head_bias[:, 0 : head_bias_ref.shape[1]] = head_bias_ref[...]
    used = 2 * lines
    for block in range(CHS):
        point_w[block * WIDE + used : (block + 1) * WIDE, :] = jnp.zeros(
            (WIDE - used, chans), jnp.bfloat16
        )
    pl.semaphore_wait(barrier, SEQ * CHS - 1)

    for copy in own_layer():
        copy.start()
    small_copies = [
        remote(
            small.at[ch], small.at[ch], s_send.at[number], s_recv.at[number], (seq, peer)
        )
        for number, peer in enumerate((across, sibling, diagonal))
    ]
    for copy in small_copies:
        copy.start()
    stream_sends(start_early)
    each_layer(start_layer)
    tracks = head_ref.shape[1]
    edge = tracks // 128 * 128
    pack_head[:, edge:] = jnp.zeros((depth, HEADW - edge), jnp.bfloat16)
    pack_head[:, 0:tracks] = head_ref[...]

    @pl.when(seq == first_seq)
    def _():
        own_head().start()

    @pl.when(seq != first_seq)
    def _():
        head_copy().start()

    past[0:256, :] = jnp.zeros((256, past.shape[1]), jnp.float32)
    past_x[0:128, :] = jnp.zeros((128, chans), jnp.float32)

    @pl.when(seq == first_seq)
    def _():
        slots = slot_ref.shape[1]

        @pl.when(ch == CHS - 1)
        def _():
            for chunk in range((SEQ * rows - STEP * (CHS - 1)) // TILE, CHUNKS):
                inbox[chunk] = jnp.zeros((TILE, chans), jnp.bfloat16)

        @pl.loop(0, GROUPS - IDLE)
        def _(group):
            place_in = lax.broadcasted_iota(
                jnp.int32, (CHS * GROUP, start_ref.shape[1]), 0
            )
            quarter = place_in // GROUP
            local_row = (group + IDLE) * GROUP + place_in % GROUP
            bins = quarter * STEP + local_row - (2**LAYERS - 1)
            least = 255 + 256 * jnp.minimum(quarter, 1)
            owned_bin = (local_row >= least) & (local_row < GROUPS * GROUP - 1)
            member = (
                (bins >= start_ref[...])
                & (bins < start_ref[...] + length_ref[...])
                & owned_bin
            )
            names = lax.broadcasted_iota(jnp.int32, (slots, owner_ref.shape[1]), 0)
            owned = lax.dot_general(
                jnp.where(names == owner_ref[...], 1.0, 0.0).astype(jnp.bfloat16),
                jnp.where(member, 1.0, 0.0).astype(jnp.bfloat16),
                (((1,), (1,)), ((), ())),
                preferred_element_type=jnp.float32,
            )
            order = lax.broadcasted_iota(jnp.int32, (slots, slots), 0) == slot_ref[...]
            counts[group] = jnp.dot(
                jnp.where(order, 1.0, 0.0).astype(jnp.bfloat16),
                owned.astype(jnp.bfloat16),
                preferred_element_type=jnp.float32,
            ).astype(jnp.bfloat16)

    def arrive(number, origin):
        block = (ch, across, sibling, diagonal)[number]
        for part, spot in ((0, conv_spot(origin, block)), (1, point_spot(origin, block))):
            remote(
                spot, spot, f_send.at[0, 0, 0], w_recv.at[number, origin, part], (seq, sibling)
            ).wait_recv()

    def forward(number, origin, kind):
        block = (ch, across)[number]
        peer, arrival = ((across, 1), (sibling, 2), (sibling, 3))[kind]
        return [
            remote(
                spot,
                spot,
                f_send.at[kind, origin, part],
                w_recv.at[arrival, origin, part],
                (seq, peer),
            )
            for part, spot in (
                (0, conv_spot(origin, block)),
                (1, point_spot(origin, block)),
            )
        ]

    def across_too(origin):
        return (stage >= BOTH) | (origin == seq)

    def take_direct(origin):
        arrive(0, origin)

        @pl.when(across_too(origin))
        def _():
            for copy in forward(0, origin, 0):
                copy.start()

        for copy in forward(0, origin, 1):
            copy.start()

    def take_across(origin):
        arrive(1, origin)
        for copy in forward(1, origin, 2):
            copy.start()

    origins = [at_place(place + offset) for offset in OFFSETS]
    for number, origin in enumerate(origins):
        take_direct(origin)
        if number:
            take_across(origins[number - 1])
    take_across(origins[-1])
    for copy in small_copies:
        copy.wait_recv()
    for block in range(CHS):
        conv_bias[:, block * WIDE : (block + 1) * WIDE] = small[block, pl.ds(stage, 1), 0:WIDE]
        point_bias[:, block * width : (block + 1) * width] = small[
            block, pl.ds(stage, 1), WIDE : WIDE + width
        ]
    for origin in origins:
        arrive(2, origin)
        arrive(3, origin)
    stream_sends(start_late)


    spread = 1
    for number in range(1, SEQ):
        spread = spread + (2 ** (number - 1)) * jnp.where(stage >= number, 1, 0)
    after = at_place(place + 1)

    def norm_rows(slot, turn, first, count):
        wide = inbox[slot, pl.ds(first, count), :].astype(jnp.float32)
        squares = jnp.sum(wide * wide, axis=1, keepdims=True)
        scale = lax.rsqrt(squares / chans + 1e-06)
        return wide, wide * scale * gain_ref[pl.ds(turn, 1), :]

    def hop(chunk):
        landing = chunk + CHUNKS * jnp.where(stage == SEQ - 1, 1, 0)
        return remote(
            outbox.at[chunk], inbox.at[landing], x_send.at[chunk], x_recv.at[landing], (after, ch)
        )

    def inbox_arrive(slot):
        remote(
            inbox.at[slot], inbox.at[slot], x_send.at[0], x_recv.at[slot], (after, ch)
        ).wait_recv()

    sub = 16

    def pass_stream(chunk):
        return remote(
            inbox.at[chunk],
            inbox.at[chunk + STEP // TILE],
            e_send.at[chunk],
            x_recv.at[chunk + STEP // TILE],
            (seq, sibling),
        )

    passing = (seq == first_seq) & (ch % 2 == 1)

    def shifted(ref, base, lag, lanes):
        steps = (lag + 7) // 8
        window = ref[pl.ds(pl.multiple_of(base - steps * 8, 8), TILE + 8), lanes]
        turn = (TILE + 8 - steps * 8 + lag) % (TILE + 8)
        return pltpu.roll(window, turn, 0)[0:TILE]

    def run_chunk(chunk):
        base = pl.multiple_of(chunk * TILE, TILE)

        absent = (seq == first_seq) & (
            ch * STEP + chunk * TILE >= SEQ * rows
        )

        @pl.when(jnp.logical_not(absent))
        def _():
            inbox_arrive(chunk)

        @pl.when(passing & (chunk < CHUNKS - STEP // TILE))
        def _():
            pass_stream(chunk).start()

        for first in range(0, TILE, sub):
            wide, normed = norm_rows(chunk, stage, first, sub)
            bins = (
                ch * STEP
                + chunk * TILE
                + first
                - (spread - 1)
                + lax.broadcasted_iota(jnp.int32, (sub, chans), 0)
            )
            inside = (bins >= 0) & (bins < SEQ * rows)
            act[first : first + sub, :] = jnp.where(inside, gelu(normed), 0.0).astype(
                jnp.bfloat16
            )
            past_x[pl.ds(128 + base + first, sub), :] = wide
        for block in range(CHS):
            taps = jnp.dot(
                act[...],
                conv_w[:, block * CONV : (block + 1) * CONV],
                preferred_element_type=jnp.float32,
            )
            lane = block * KEPT
            past[pl.ds(256 + base, TILE), lane : lane + KEPT] = taps[:, 0:KEPT]
            far, near = 2 * spread, spread
            left = (
                shifted(past, 256 + base, far, slice(lane, lane + 128))
                + shifted(past, 256 + base, near, slice(lane + 128, lane + 256))
                + taps[:, KEPT : KEPT + 128]
                + conv_bias[:, block * WIDE : block * WIDE + 128]
            )
            right = (
                shifted(past, 256 + base, far, slice(lane + 256, lane + 384))
                + pltpu.roll(shifted(past, 256 + base, near, slice(lane + 256, lane + 384)), 64, 1)
                + taps[:, KEPT + 128 : CONV]
                + conv_bias[:, block * WIDE + 128 : (block + 1) * WIDE]
            )
            hid[:, block * WIDE : block * WIDE + 128] = gelu(left).astype(jnp.bfloat16)
            hid[:, block * WIDE + 128 : (block + 1) * WIDE] = gelu(right).astype(jnp.bfloat16)
        for block in range(CHS):
            lanes = slice(block * width, (block + 1) * width)
            mixed = jnp.dot(hid[...], point_w[:, lanes], preferred_element_type=jnp.float32)
            outbox[chunk, :, lanes] = (
                shifted(past_x, 128 + base, spread, lanes) + mixed + point_bias[:, lanes]
            ).astype(jnp.bfloat16)
        hop(chunk).start()

    @pl.loop(0, CHUNKS)
    def _(chunk):
        run_chunk(chunk)

    def total_copy(origin):
        return remote(
            total.at[pl.ds(origin * 8, 8)],
            landed,
            t_send.at[origin],
            t_recv,
            (origin, ch),
        )

    def final_copies(group):
        def copy(block, peer, number):
            return remote(
                finals.at[group, block],
                finals.at[group, block],
                g_send.at[number, group],
                g_recv.at[number, group],
                (seq, peer),
            )

        return copy(ch, across, 0), copy(ch, sibling, 1), copy(across, sibling, 2)

    def pass_on(group):
        to_across, _, onward = final_copies(group)
        to_across.wait_recv()
        onward.start()

    def give_group(group, between=None):
        for part in range(GROUP // TILE):
            slot = CHUNKS + (group + IDLE) * (GROUP // TILE) + part
            inbox_arrive(slot)
            if part == 0 and between is not None:
                between()
            for first in range(0, TILE, sub):
                _, normed = norm_rows(slot, LAYERS, first, sub)
                start = part * TILE + first
                finals[group, ch, start : start + sub, :] = normed.astype(jnp.bfloat16)
        to_across, to_sibling, _ = final_copies(group)
        to_across.start()
        to_sibling.start()

    def take_group(group):
        _, to_sibling, onward = final_copies(group)
        to_sibling.wait_recv()
        onward.wait_recv()
        rows_in = finals[group].reshape(CHS * GROUP, chans)
        for start in range(0, HEADW, 256):
            lanes = slice(start, start + 256)
            logits = (
                jnp.dot(rows_in, head_w[:, lanes], preferred_element_type=jnp.float32)
                + head_bias[:, lanes]
            )
            cover = jnp.maximum(logits, 0.0) + jnp.log1p(jnp.exp(-jnp.abs(logits)))
            sums = total[:, lanes]
            for _ in range(3):
                piece = cover.astype(jnp.bfloat16)
                sums = sums + jnp.dot(
                    counts[group], piece, preferred_element_type=jnp.float32
                )
                cover = cover - piece.astype(jnp.float32)
            total[:, lanes] = sums

    @pl.when(seq == first_seq)
    def _():
        for origin in origins:
            head_copy_in = remote(
                pack_head, head_spot(origin), h_send, h_recv.at[origin], (seq, sibling)
            )
            head_copy_in.wait_recv()
        total[...] = jnp.zeros_like(total)

        @pl.loop(0, IDLE * GROUP // TILE)
        def _(chunk):
            inbox_arrive(CHUNKS + chunk)

        give_group(0)

        @pl.loop(1, GROUPS - IDLE)
        def _(group):
            give_group(group, lambda: pass_on(group - 1))
            take_group(group - 1)

        pass_on(GROUPS - IDLE - 1)
        take_group(GROUPS - IDLE - 1)
        for origin in range(SEQ):

            @pl.when(origin == first_seq)
            def _():
                pltpu.make_async_copy(total.at[pl.ds(origin * 8, 8)], landed, t_recv).start()

            @pl.when(origin != first_seq)
            def _():
                total_copy(origin).start()

    each_layer(finish_layer)

    @pl.when(seq != first_seq)
    def _():
        head_copy().wait_send()

    stream_sends(finish_stream)
    for copy in small_copies:
        copy.wait_send()
    for origin in origins:

        @pl.when(across_too(origin))
        def _():
            for copy in forward(0, origin, 0):
                copy.wait_send()

        for copy in forward(0, origin, 1) + forward(1, origin, 2):
            copy.wait_send()

    @pl.loop(0, CHUNKS)
    def _(chunk):
        hop(chunk).wait_send()

        @pl.when(passing & (chunk < CHUNKS - STEP // TILE))
        def _():
            pass_stream(chunk).wait_send()

    remote(landed, landed, t_send.at[0], t_recv, (seq, sibling)).wait_recv()
    out_ref[...] = jnp.log1p(landed[...])[:, : out_ref.shape[1]]

    @pl.when(seq == first_seq)
    def _():
        @pl.loop(0, GROUPS - IDLE)
        def _(group):
            for copy in final_copies(group):
                copy.wait_send()

        for origin in range(SEQ):

            @pl.when(origin != first_seq)
            def _():
                total_copy(origin).wait_send()


def local_kernel(
    stream,
    norm_gain,
    conv_weight,
    conv_bias,
    point_weight,
    point_bias,
    head_weight,
    head_bias,
    exon_start,
    exon_length,
    exon_transcript,
    transcript_slot,
):
    rows, width = stream.shape
    depth = conv_weight.shape[2]
    tracks = head_weight.shape[1]
    slots = transcript_slot.shape[0]
    chans = CHS * width
    vmem = pl.BlockSpec(memory_space=pltpu.VMEM)
    dma = pltpu.SemaphoreType.DMA
    f32, bf16 = jnp.float32, jnp.bfloat16
    return pl.pallas_call(
        tower_kernel,
        out_shape=jax.ShapeDtypeStruct((slots // SEQ, tracks), f32),
        in_specs=[vmem] * 12,
        out_specs=vmem,
        scratch_shapes=[
            pltpu.VMEM((LAYERS, depth, CONV), bf16),
            pltpu.VMEM((depth, HEADW), bf16),
            pltpu.VMEM((chans, CHS * CONV), bf16),
            pltpu.VMEM((CHS * WIDE, chans), bf16),
            pltpu.VMEM((chans, HEADW), bf16),
            pltpu.VMEM((CHS, 8, 640), f32),
            pltpu.VMEM((2 * CHUNKS, TILE, chans), bf16),
            pltpu.VMEM((CHUNKS, TILE, chans), bf16),
            pltpu.VMEM((264 + CHUNKS * TILE, CHS * KEPT), f32),
            pltpu.VMEM((136 + CHUNKS * TILE, chans), f32),
            pltpu.VMEM((TILE, chans), bf16),
            pltpu.VMEM((TILE, CHS * WIDE), bf16),
            pltpu.VMEM((GROUPS - IDLE, slots, CHS * GROUP), bf16),
            pltpu.VMEM((1, CHS * WIDE), f32),
            pltpu.VMEM((1, chans), f32),
            pltpu.VMEM((1, HEADW), f32),
            pltpu.VMEM((GROUPS - IDLE, CHS, GROUP, chans), bf16),
            pltpu.VMEM((slots, HEADW), f32),
            pltpu.VMEM((slots // SEQ, HEADW), f32),
            dma((2, LAYERS, 2)),
            dma((4, SEQ, 2)),
            dma((3, SEQ, 2)),
            dma(()),
            dma((SEQ,)),
            dma((3, GROUPS - IDLE)),
            dma((3, GROUPS - IDLE)),
            dma((3,)),
            dma((3,)),
            dma((CHUNKS,)),
            dma((2 * CHUNKS,)),
            dma((CHS, rows // TILE)),
            dma((CHUNKS - STEP // TILE,)),
            dma((SEQ,)),
            dma(()),
        ],
        compiler_params=pltpu.CompilerParams(
            collective_id=0, has_side_effects=True, vmem_limit_bytes=60 * 2**20
        ),
        cost_estimate=pl.CostEstimate(
            flops=20_000_000_000, bytes_accessed=4_000_000, transcendentals=8_000_000
        ),
    )(
        stream,
        norm_gain,
        conv_weight,
        conv_bias,
        point_weight,
        point_bias,
        head_weight,
        head_bias[None, :],
        exon_start[None, :],
        exon_length[None, :],
        exon_transcript[None, :],
        transcript_slot[None, :],
    )


def local(*args):
    stream, conv_weight, point_weight, head_weight = args[0], args[2], args[4], args[6]
    fits = (
        lax.axis_size("seq") == SEQ
        and lax.axis_size("ch") == CHS
        and stream.shape == (256, 384)
        and conv_weight.shape[1:] == (3, 192, 192)
        and point_weight.shape[1:] == (96, 384)
        and head_weight.shape == (192, 960)
        and args[11].shape[0] == 8 * SEQ
    )
    return local_kernel(*args) if fits else local_plain(*args)


def solution(mesh):
    placed = (
        P("seq", "ch"),
        P(),
        P(None, None, "seq", "ch"),
        P(None, "ch"),
        P(None, "seq", "ch"),
        P(None, "ch"),
        P("seq", "ch"),
        P("ch"),
        P(),
        P(),
        P(),
        P(),
    )
    return jax.shard_map(
        local, mesh=mesh, in_specs=placed, out_specs=P("seq", "ch"), check_vma=False
    )
```

```python
import jax
import jax.numpy as jnp
from jax import lax
from jax.experimental import pallas as pl
from jax.experimental.pallas import tpu as pltpu
from jax.sharding import PartitionSpec as P

LAYERS = 8


def padded(block, sides, width):
    for axis, dim in sides:
        count = lax.axis_size(axis)
        forward = [(i, i + 1) for i in range(count - 1)]
        backward = [(target, source) for source, target in forward]
        low = lax.ppermute(
            lax.slice_in_dim(block, block.shape[dim] - width, None, axis=dim), axis, forward
        )
        high = lax.ppermute(lax.slice_in_dim(block, 0, width, axis=dim), axis, backward)
        block = jnp.concatenate([low, block, high], axis=dim)
    return block


def rms_scaled(values, gain_row):
    wide = values.astype(jnp.float32)
    scale = lax.rsqrt(jnp.mean(wide * wide, axis=-1, keepdims=True) + 1e-06)
    return wide * scale * gain_row


def local_plain(
    stream,
    norm_gain,
    conv_weight,
    conv_bias,
    point_weight,
    point_bias,
    head_weight,
    head_bias,
    exon_start,
    exon_length,
    exon_transcript,
    transcript_slot,
):
    bin_rows = stream.shape[0]
    resid = stream
    for layer_idx in range(LAYERS):
        spread = 2**layer_idx
        rimmed = padded(resid, (("seq", 0),), spread)
        full_rows = lax.all_gather(rimmed, "ch", axis=1, tiled=True)
        act_rows = jax.nn.gelu(
            rms_scaled(full_rows, norm_gain[layer_idx]), approximate=False
        ).astype(jnp.bfloat16)
        tap_rows = jnp.stack(
            [
                act_rows[0:bin_rows],
                act_rows[spread : spread + bin_rows],
                act_rows[2 * spread : 2 * spread + bin_rows],
            ]
        )
        conv_sum = jnp.einsum(
            "kbc,kch->bh",
            tap_rows,
            lax.all_gather(conv_weight[layer_idx], "seq", axis=1, tiled=True),
            preferred_element_type=jnp.float32,
        )
        hidden = jax.nn.gelu(conv_sum + conv_bias[layer_idx], approximate=False).astype(
            jnp.bfloat16
        )
        hidden_all = lax.all_gather(hidden, "ch", axis=1, tiled=True)
        mixed = jnp.dot(
            hidden_all,
            lax.all_gather(point_weight[layer_idx], "seq", axis=0, tiled=True),
            preferred_element_type=jnp.float32,
        )
        resid = (resid.astype(jnp.float32) + mixed + point_bias[layer_idx]).astype(jnp.bfloat16)
    final_all = lax.all_gather(resid, "ch", axis=1, tiled=True)
    final_rows = rms_scaled(final_all, norm_gain[LAYERS]).astype(jnp.bfloat16)
    logits = jnp.dot(
        final_rows,
        lax.all_gather(head_weight, "seq", axis=0, tiled=True),
        preferred_element_type=jnp.float32,
    )
    coverage = jax.nn.softplus(logits + head_bias)
    seq_index = lax.axis_index("seq")
    bin_ids = seq_index * bin_rows + jnp.arange(bin_rows, dtype=jnp.int32)
    member = (
        (bin_ids[None, :] >= exon_start[:, None])
        & (bin_ids[None, :] < (exon_start + exon_length)[:, None])
    ).astype(jnp.bfloat16)
    owner_rows = transcript_slot[exon_transcript]
    select = (
        owner_rows[None, :] == jnp.arange(transcript_slot.shape[0], dtype=jnp.int32)[:, None]
    ).astype(jnp.bfloat16)
    counts = jnp.dot(select, member, preferred_element_type=jnp.float32)
    total = lax.psum_scatter(
        jnp.dot(counts, coverage, precision=lax.Precision.HIGHEST),
        "seq",
        scatter_dimension=0,
        tiled=True,
    )
    return jnp.log1p(total)


SEQ = 8
CHS = 4
BOTH = 0
START = 2
TILE = 32
CHUNKS = 960 // TILE
GROUP = 160
GROUPS = 960 // GROUP
IDLE = 1
LATE = 511 // GROUP - IDLE
EARLY = 192 // TILE
STEP = 448
CONV = 640
KEPT = 384
WIDE = 256
HEADW = 1024
MESH = pl.DeviceIdType.MESH
OFFSETS = (0, 1, -1, 2, -2, 3, -3, 4)


def gelu(values):
    return 0.5 * values * (1.0 + lax.erf(values * 0.7071067811865476))


def at_place(spot):
    spot = (spot + 2 * SEQ) % SEQ
    upper = spot // (SEQ // 2)
    return (1 - upper) * 2 * spot + upper * (2 * (SEQ - 1 - spot) + 1)


def tower_kernel(
    x_ref,
    gain_ref,
    conv_ref,
    conv_bias_ref,
    point_ref,
    point_bias_ref,
    head_ref,
    head_bias_ref,
    start_ref,
    length_ref,
    owner_ref,
    slot_ref,
    out_ref,
    pack_conv,
    pack_head,
    conv_w,
    point_w,
    head_w,
    small,
    inbox,
    outbox,
    past,
    past_x,
    act,
    hid,
    counts,
    conv_bias,
    point_bias,
    head_bias,
    finals,
    total,
    landed,
    w_send,
    w_recv,
    f_send,
    h_send,
    h_recv,
    g_send,
    g_recv,
    s_send,
    s_recv,
    x_send,
    x_recv,
    c_send,
    e_send,
    t_send,
    t_recv,
):
    seq = lax.axis_index("seq")
    ch = lax.axis_index("ch")
    odd = seq % 2
    place = (1 - odd) * (seq // 2) + odd * (SEQ - 1 - seq // 2)
    stage = (place - START + SEQ) % SEQ
    sibling = ch + 1 - 2 * (ch % 2)
    across = (ch + 2) % CHS
    diagonal = (sibling + 2) % CHS
    first_seq = at_place(START)
    rows, width = x_ref.shape
    chans = width * CHS
    depth = conv_ref.shape[2]
    lines = point_ref.shape[1]

    barrier = pltpu.get_barrier_semaphore()

    @pl.loop(1, SEQ * CHS)
    def _(step):
        peer = (seq * CHS + ch + step) % (SEQ * CHS)
        pl.semaphore_signal(
            barrier, inc=1, device_id=(peer // CHS, peer % CHS), device_id_type=MESH
        )

    def remote(src, dst, send, recv, target):
        return pltpu.make_async_remote_copy(
            src_ref=src,
            dst_ref=dst,
            send_sem=send,
            recv_sem=recv,
            device_id=target,
            device_id_type=MESH,
        )

    def conv_spot(origin, block):
        return conv_w.at[
            pl.ds(pl.multiple_of(origin * depth, 64), depth),
            pl.ds(pl.multiple_of(block * CONV, 128), CONV),
        ]

    def point_spot(origin, block):
        row = (origin // 2) * WIDE + (origin % 2) * lines
        return point_w.at[
            pl.ds(pl.multiple_of(row, 32), lines),
            pl.ds(pl.multiple_of(block * width, 128), width),
        ]

    def head_spot(origin):
        return head_w.at[pl.ds(pl.multiple_of(origin * depth, 64), depth)]

    def pack(layer):
        taps = [conv_ref[layer, tap] for tap in range(3)]
        own = pack_conv.at[layer]
        own[:, 0:128] = taps[0][:, 0:128]
        own[:, 128:256] = taps[1][:, 0:128]
        own[:, 256:384] = jnp.concatenate([taps[0][:, 128:192], taps[1][:, 128:192]], axis=1)
        own[:, 384:512] = taps[2][:, 0:128]
        own[:, 512:640] = jnp.concatenate(
            [taps[2][:, 128:192], jnp.zeros((depth, 64), jnp.bfloat16)], axis=1
        )

    def layer_copies(layer, peer, number):
        target = (at_place(layer + START), peer)
        return (
            remote(
                pack_conv.at[layer],
                conv_spot(seq, ch),
                w_send.at[number, layer, 0],
                w_recv.at[number, seq, 0],
                target,
            ),
            remote(
                point_ref.at[layer],
                point_spot(seq, ch),
                w_send.at[number, layer, 1],
                w_recv.at[number, seq, 1],
                target,
            ),
        )

    def own_layer():
        return (
            pltpu.make_async_copy(
                pack_conv.at[stage], conv_spot(seq, ch), w_recv.at[0, seq, 0]
            ),
            pltpu.make_async_copy(
                point_ref.at[stage], point_spot(seq, ch), w_recv.at[0, seq, 1]
            ),
        )

    def each_layer(act_on):
        for offset in OFFSETS[1:]:
            layer = (stage + offset + SEQ) % SEQ
            act_on(layer, layer_copies(layer, ch, 0))

            @pl.when(layer < BOTH)
            def _():
                act_on(None, layer_copies(layer, across, 1))

    def start_layer(layer, copies):
        if layer is not None:
            pack(layer)
        for copy in copies:
            copy.start()

    def finish_layer(layer, copies):
        for copy in copies:
            copy.wait_send()

    def head_copy():
        return remote(pack_head, head_spot(seq), h_send, h_recv.at[seq], (first_seq, ch))

    def own_head():
        return pltpu.make_async_copy(pack_head, head_spot(seq), h_recv.at[seq])

    def stream_sends(act_on):
        parts = rows // TILE
        for dest in range(CHS):
            for part in range(parts):
                chunk = seq * parts + part - (STEP // TILE) * dest
                inside = (chunk >= 0) & (chunk < (CHUNKS if dest % 2 else STEP // TILE))
                chunk_at = jnp.clip(chunk, 0, CHUNKS - 1)
                mine = (seq == first_seq) & (ch == dest)
                src = x_ref.at[pl.ds(part * TILE, TILE)]
                dst = inbox.at[
                    chunk_at, :, pl.ds(pl.multiple_of(ch * width, 128), width)
                ]
                act_on(dest, part, inside, mine, chunk_at, src, dst)

    def start_early(dest, part, inside, *rest):
        start_stream(dest, part, inside & (rest[1] < EARLY), *rest)

    def start_late(dest, part, inside, *rest):
        start_stream(dest, part, inside & (rest[1] >= EARLY), *rest)

    def start_stream(dest, part, inside, mine, chunk, src, dst):
        @pl.when(inside & mine)
        def _():
            pltpu.make_async_copy(src, dst, x_recv.at[chunk]).start()

        @pl.when(inside & jnp.logical_not(mine))
        def _():
            remote(
                src, dst, c_send.at[dest, part], x_recv.at[chunk], (first_seq, dest)
            ).start()

    def finish_stream(dest, part, inside, mine, chunk, src, dst):
        @pl.when(inside & jnp.logical_not(mine))
        def _():
            remote(
                src, dst, c_send.at[dest, part], x_recv.at[chunk], (first_seq, dest)
            ).wait_send()

    pack(stage)
    own_small = small.at[ch]
    own_small[...] = jnp.zeros(own_small.shape, jnp.float32)
    own_small[0:LAYERS, 0 : conv_bias_ref.shape[1]] = conv_bias_ref[...]
    own_small[0:LAYERS, WIDE : WIDE + width] = point_bias_ref[...]
    head_bias[...] = jnp.zeros_like(head_bias)
    head_bias[:, 0 : head_bias_ref.shape[1]] = head_bias_ref[...]
    used = 2 * lines
    for block in range(CHS):
        point_w[block * WIDE + used : (block + 1) * WIDE, :] = jnp.zeros(
            (WIDE - used, chans), jnp.bfloat16
        )
    pl.semaphore_wait(barrier, SEQ * CHS - 1)

    for copy in own_layer():
        copy.start()
    small_copies = [
        remote(
            small.at[ch], small.at[ch], s_send.at[number], s_recv.at[number], (seq, peer)
        )
        for number, peer in enumerate((across, sibling, diagonal))
    ]
    for copy in small_copies:
        copy.start()
    stream_sends(start_early)
    each_layer(start_layer)
    tracks = head_ref.shape[1]
    edge = tracks // 128 * 128
    pack_head[:, edge:] = jnp.zeros((depth, HEADW - edge), jnp.bfloat16)
    pack_head[:, 0:tracks] = head_ref[...]

    @pl.when(seq == first_seq)
    def _():
        own_head().start()

    @pl.when(seq != first_seq)
    def _():
        head_copy().start()

    past[0:256, :] = jnp.zeros((256, past.shape[1]), jnp.float32)
    past_x[0:128, :] = jnp.zeros((128, chans), jnp.float32)

    @pl.when(seq == first_seq)
    def _():
        slots = slot_ref.shape[1]

        @pl.when(ch == CHS - 1)
        def _():
            for chunk in range((SEQ * rows - STEP * (CHS - 1)) // TILE, CHUNKS):
                inbox[chunk] = jnp.zeros((TILE, chans), jnp.bfloat16)

        for group in range(LATE):
            for block in range(1, CHS):
                finals[group, block] = jnp.zeros((GROUP, chans), jnp.bfloat16)

        @pl.loop(0, GROUPS - IDLE)
        def _(group):
            place_in = lax.broadcasted_iota(
                jnp.int32, (CHS * GROUP, start_ref.shape[1]), 0
            )
            quarter = place_in // GROUP
            local_row = (group + IDLE) * GROUP + place_in % GROUP
            bins = quarter * STEP + local_row - (2**LAYERS - 1)
            least = 255 + 256 * jnp.minimum(quarter, 1)
            owned_bin = (local_row >= least) & (local_row < GROUPS * GROUP - 1)
            member = (
                (bins >= start_ref[...])
                & (bins < start_ref[...] + length_ref[...])
                & owned_bin
            )
            names = lax.broadcasted_iota(jnp.int32, (slots, owner_ref.shape[1]), 0)
            owned = lax.dot_general(
                jnp.where(names == owner_ref[...], 1.0, 0.0).astype(jnp.bfloat16),
                jnp.where(member, 1.0, 0.0).astype(jnp.bfloat16),
                (((1,), (1,)), ((), ())),
                preferred_element_type=jnp.float32,
            )
            order = lax.broadcasted_iota(jnp.int32, (slots, slots), 0) == slot_ref[...]
            counts[group] = jnp.dot(
                jnp.where(order, 1.0, 0.0).astype(jnp.bfloat16),
                owned.astype(jnp.bfloat16),
                preferred_element_type=jnp.float32,
            ).astype(jnp.bfloat16)

    def arrive(number, origin):
        block = (ch, across, sibling, diagonal)[number]
        for part, spot in ((0, conv_spot(origin, block)), (1, point_spot(origin, block))):
            remote(
                spot, spot, f_send.at[0, 0, 0], w_recv.at[number, origin, part], (seq, sibling)
            ).wait_recv()

    def forward(number, origin, kind):
        block = (ch, across)[number]
        peer, arrival = ((across, 1), (sibling, 2), (sibling, 3))[kind]
        return [
            remote(
                spot,
                spot,
                f_send.at[kind, origin, part],
                w_recv.at[arrival, origin, part],
                (seq, peer),
            )
            for part, spot in (
                (0, conv_spot(origin, block)),
                (1, point_spot(origin, block)),
            )
        ]

    def across_too(origin):
        return (stage >= BOTH) | (origin == seq)

    def take_direct(origin):
        arrive(0, origin)

        @pl.when(across_too(origin))
        def _():
            for copy in forward(0, origin, 0):
                copy.start()

        for copy in forward(0, origin, 1):
            copy.start()

    def take_across(origin):
        arrive(1, origin)
        for copy in forward(1, origin, 2):
            copy.start()

    origins = [at_place(place + offset) for offset in OFFSETS]
    for number, origin in enumerate(origins):
        take_direct(origin)
        if number:
            take_across(origins[number - 1])
    take_across(origins[-1])
    for copy in small_copies:
        copy.wait_recv()
    for block in range(CHS):
        conv_bias[:, block * WIDE : (block + 1) * WIDE] = small[block, pl.ds(stage, 1), 0:WIDE]
        point_bias[:, block * width : (block + 1) * width] = small[
            block, pl.ds(stage, 1), WIDE : WIDE + width
        ]
    for origin in origins:
        arrive(2, origin)
        arrive(3, origin)
    stream_sends(start_late)


    spread = 1
    for number in range(1, SEQ):
        spread = spread + (2 ** (number - 1)) * jnp.where(stage >= number, 1, 0)
    after = at_place(place + 1)

    def norm_rows(slot, turn, first, count):
        wide = inbox[slot, pl.ds(first, count), :].astype(jnp.float32)
        squares = jnp.sum(wide * wide, axis=1, keepdims=True)
        scale = lax.rsqrt(squares / chans + 1e-06)
        return wide, wide * scale * gain_ref[pl.ds(turn, 1), :]

    def hop(chunk):
        landing = chunk + CHUNKS * jnp.where(stage == SEQ - 1, 1, 0)
        return remote(
            outbox.at[chunk], inbox.at[landing], x_send.at[chunk], x_recv.at[landing], (after, ch)
        )

    def inbox_arrive(slot):
        remote(
            inbox.at[slot], inbox.at[slot], x_send.at[0], x_recv.at[slot], (after, ch)
        ).wait_recv()

    sub = 16

    def pass_stream(chunk):
        return remote(
            inbox.at[chunk],
            inbox.at[chunk + STEP // TILE],
            e_send.at[chunk],
            x_recv.at[chunk + STEP // TILE],
            (seq, sibling),
        )

    passing = (seq == first_seq) & (ch % 2 == 1)

    def shifted(ref, base, lag, lanes):
        steps = (lag + 7) // 8
        window = ref[pl.ds(pl.multiple_of(base - steps * 8, 8), TILE + 8), lanes]
        turn = (TILE + 8 - steps * 8 + lag) % (TILE + 8)
        return pltpu.roll(window, turn, 0)[0:TILE]

    def run_chunk(chunk):
        base = pl.multiple_of(chunk * TILE, TILE)

        absent = (seq == first_seq) & (
            ch * STEP + chunk * TILE >= SEQ * rows
        )

        @pl.when(jnp.logical_not(absent))
        def _():
            inbox_arrive(chunk)

        @pl.when(passing & (chunk < CHUNKS - STEP // TILE))
        def _():
            pass_stream(chunk).start()

        for first in range(0, TILE, sub):
            wide, normed = norm_rows(chunk, stage, first, sub)
            bins = (
                ch * STEP
                + chunk * TILE
                + first
                - (spread - 1)
                + lax.broadcasted_iota(jnp.int32, (sub, chans), 0)
            )
            inside = (bins >= 0) & (bins < SEQ * rows)
            act[first : first + sub, :] = jnp.where(inside, gelu(normed), 0.0).astype(
                jnp.bfloat16
            )
            past_x[pl.ds(128 + base + first, sub), :] = wide
        for block in range(CHS):
            taps = jnp.dot(
                act[...],
                conv_w[:, block * CONV : (block + 1) * CONV],
                preferred_element_type=jnp.float32,
            )
            lane = block * KEPT
            past[pl.ds(256 + base, TILE), lane : lane + KEPT] = taps[:, 0:KEPT]
            far, near = 2 * spread, spread
            left = (
                shifted(past, 256 + base, far, slice(lane, lane + 128))
                + shifted(past, 256 + base, near, slice(lane + 128, lane + 256))
                + taps[:, KEPT : KEPT + 128]
                + conv_bias[:, block * WIDE : block * WIDE + 128]
            )
            right = (
                shifted(past, 256 + base, far, slice(lane + 256, lane + 384))
                + pltpu.roll(shifted(past, 256 + base, near, slice(lane + 256, lane + 384)), 64, 1)
                + taps[:, KEPT + 128 : CONV]
                + conv_bias[:, block * WIDE + 128 : (block + 1) * WIDE]
            )
            hid[:, block * WIDE : block * WIDE + 128] = gelu(left).astype(jnp.bfloat16)
            hid[:, block * WIDE + 128 : (block + 1) * WIDE] = gelu(right).astype(jnp.bfloat16)
        for block in range(CHS):
            lanes = slice(block * width, (block + 1) * width)
            mixed = jnp.dot(hid[...], point_w[:, lanes], preferred_element_type=jnp.float32)
            outbox[chunk, :, lanes] = (
                shifted(past_x, 128 + base, spread, lanes) + mixed + point_bias[:, lanes]
            ).astype(jnp.bfloat16)
        hop(chunk).start()

    @pl.loop(0, CHUNKS)
    def _(chunk):
        run_chunk(chunk)

    def total_copy(origin):
        return remote(
            total.at[pl.ds(origin * 8, 8)],
            landed,
            t_send.at[origin],
            t_recv,
            (origin, ch),
        )

    def final_copies(group):
        def copy(block, peer, number):
            return remote(
                finals.at[group, block],
                finals.at[group, block],
                g_send.at[number, group],
                g_recv.at[number, group],
                (seq, peer),
            )

        return copy(ch, across, 0), copy(ch, sibling, 1), copy(across, sibling, 2)

    def needed(block, group):
        return (block == 0) | (group >= LATE)

    def pass_on(group):
        to_across, _, onward = final_copies(group)

        @pl.when(needed(across, group))
        def _():
            to_across.wait_recv()
            onward.start()

    def give_group(group, between=None):
        for part in range(GROUP // TILE):
            slot = CHUNKS + (group + IDLE) * (GROUP // TILE) + part
            inbox_arrive(slot)
            if part == 0 and between is not None:
                between()
            for first in range(0, TILE, sub):
                _, normed = norm_rows(slot, LAYERS, first, sub)
                start = part * TILE + first
                finals[group, ch, start : start + sub, :] = normed.astype(jnp.bfloat16)
        to_across, to_sibling, _ = final_copies(group)

        @pl.when(needed(ch, group))
        def _():
            to_across.start()
            to_sibling.start()

    def take_group(group):
        _, to_sibling, onward = final_copies(group)

        @pl.when(needed(sibling, group))
        def _():
            to_sibling.wait_recv()

        @pl.when(needed(diagonal, group))
        def _():
            onward.wait_recv()

        rows_in = finals[group].reshape(CHS * GROUP, chans)
        for start in range(0, HEADW, 256):
            lanes = slice(start, start + 256)
            logits = (
                jnp.dot(rows_in, head_w[:, lanes], preferred_element_type=jnp.float32)
                + head_bias[:, lanes]
            )
            cover = jnp.maximum(logits, 0.0) + jnp.log1p(jnp.exp(-jnp.abs(logits)))
            sums = total[:, lanes]
            for _ in range(3):
                piece = cover.astype(jnp.bfloat16)
                sums = sums + jnp.dot(
                    counts[group], piece, preferred_element_type=jnp.float32
                )
                cover = cover - piece.astype(jnp.float32)
            total[:, lanes] = sums

    @pl.when(seq == first_seq)
    def _():
        for origin in origins:
            head_copy_in = remote(
                pack_head, head_spot(origin), h_send, h_recv.at[origin], (seq, sibling)
            )
            head_copy_in.wait_recv()
        total[...] = jnp.zeros_like(total)

        @pl.loop(0, IDLE * GROUP // TILE)
        def _(chunk):
            inbox_arrive(CHUNKS + chunk)

        give_group(0)

        @pl.loop(1, GROUPS - IDLE)
        def _(group):
            give_group(group, lambda: pass_on(group - 1))
            take_group(group - 1)

        pass_on(GROUPS - IDLE - 1)
        take_group(GROUPS - IDLE - 1)
        for origin in range(SEQ):

            @pl.when(origin == first_seq)
            def _():
                pltpu.make_async_copy(total.at[pl.ds(origin * 8, 8)], landed, t_recv).start()

            @pl.when(origin != first_seq)
            def _():
                total_copy(origin).start()

    each_layer(finish_layer)

    @pl.when(seq != first_seq)
    def _():
        head_copy().wait_send()

    stream_sends(finish_stream)
    for copy in small_copies:
        copy.wait_send()
    for origin in origins:

        @pl.when(across_too(origin))
        def _():
            for copy in forward(0, origin, 0):
                copy.wait_send()

        for copy in forward(0, origin, 1) + forward(1, origin, 2):
            copy.wait_send()

    @pl.loop(0, CHUNKS)
    def _(chunk):
        hop(chunk).wait_send()

        @pl.when(passing & (chunk < CHUNKS - STEP // TILE))
        def _():
            pass_stream(chunk).wait_send()

    remote(landed, landed, t_send.at[0], t_recv, (seq, sibling)).wait_recv()
    out_ref[...] = jnp.log1p(landed[...])[:, : out_ref.shape[1]]

    @pl.when(seq == first_seq)
    def _():
        @pl.loop(0, GROUPS - IDLE)
        def _(group):
            to_across, to_sibling, onward = final_copies(group)

            @pl.when(needed(ch, group))
            def _():
                to_across.wait_send()
                to_sibling.wait_send()

            @pl.when(needed(across, group))
            def _():
                onward.wait_send()

        for origin in range(SEQ):

            @pl.when(origin != first_seq)
            def _():
                total_copy(origin).wait_send()


def local_kernel(
    stream,
    norm_gain,
    conv_weight,
    conv_bias,
    point_weight,
    point_bias,
    head_weight,
    head_bias,
    exon_start,
    exon_length,
    exon_transcript,
    transcript_slot,
):
    rows, width = stream.shape
    depth = conv_weight.shape[2]
    tracks = head_weight.shape[1]
    slots = transcript_slot.shape[0]
    chans = CHS * width
    vmem = pl.BlockSpec(memory_space=pltpu.VMEM)
    dma = pltpu.SemaphoreType.DMA
    f32, bf16 = jnp.float32, jnp.bfloat16
    return pl.pallas_call(
        tower_kernel,
        out_shape=jax.ShapeDtypeStruct((slots // SEQ, tracks), f32),
        in_specs=[vmem] * 12,
        out_specs=vmem,
        scratch_shapes=[
            pltpu.VMEM((LAYERS, depth, CONV), bf16),
            pltpu.VMEM((depth, HEADW), bf16),
            pltpu.VMEM((chans, CHS * CONV), bf16),
            pltpu.VMEM((CHS * WIDE, chans), bf16),
            pltpu.VMEM((chans, HEADW), bf16),
            pltpu.VMEM((CHS, 8, 640), f32),
            pltpu.VMEM((2 * CHUNKS, TILE, chans), bf16),
            pltpu.VMEM((CHUNKS, TILE, chans), bf16),
            pltpu.VMEM((264 + CHUNKS * TILE, CHS * KEPT), f32),
            pltpu.VMEM((136 + CHUNKS * TILE, chans), f32),
            pltpu.VMEM((TILE, chans), bf16),
            pltpu.VMEM((TILE, CHS * WIDE), bf16),
            pltpu.VMEM((GROUPS - IDLE, slots, CHS * GROUP), bf16),
            pltpu.VMEM((1, CHS * WIDE), f32),
            pltpu.VMEM((1, chans), f32),
            pltpu.VMEM((1, HEADW), f32),
            pltpu.VMEM((GROUPS - IDLE, CHS, GROUP, chans), bf16),
            pltpu.VMEM((slots, HEADW), f32),
            pltpu.VMEM((slots // SEQ, HEADW), f32),
            dma((2, LAYERS, 2)),
            dma((4, SEQ, 2)),
            dma((3, SEQ, 2)),
            dma(()),
            dma((SEQ,)),
            dma((3, GROUPS - IDLE)),
            dma((3, GROUPS - IDLE)),
            dma((3,)),
            dma((3,)),
            dma((CHUNKS,)),
            dma((2 * CHUNKS,)),
            dma((CHS, rows // TILE)),
            dma((CHUNKS - STEP // TILE,)),
            dma((SEQ,)),
            dma(()),
        ],
        compiler_params=pltpu.CompilerParams(
            collective_id=0, has_side_effects=True, vmem_limit_bytes=60 * 2**20
        ),
        cost_estimate=pl.CostEstimate(
            flops=20_000_000_000, bytes_accessed=4_000_000, transcendentals=8_000_000
        ),
    )(
        stream,
        norm_gain,
        conv_weight,
        conv_bias,
        point_weight,
        point_bias,
        head_weight,
        head_bias[None, :],
        exon_start[None, :],
        exon_length[None, :],
        exon_transcript[None, :],
        transcript_slot[None, :],
    )


def local(*args):
    stream, conv_weight, point_weight, head_weight = args[0], args[2], args[4], args[6]
    fits = (
        lax.axis_size("seq") == SEQ
        and lax.axis_size("ch") == CHS
        and stream.shape == (256, 384)
        and conv_weight.shape[1:] == (3, 192, 192)
        and point_weight.shape[1:] == (96, 384)
        and head_weight.shape == (192, 960)
        and args[11].shape[0] == 8 * SEQ
    )
    return local_kernel(*args) if fits else local_plain(*args)


def solution(mesh):
    placed = (
        P("seq", "ch"),
        P(),
        P(None, None, "seq", "ch"),
        P(None, "ch"),
        P(None, "seq", "ch"),
        P(None, "ch"),
        P("seq", "ch"),
        P("ch"),
        P(),
        P(),
        P(),
        P(),
    )
    return jax.shard_map(
        local, mesh=mesh, in_specs=placed, out_specs=P("seq", "ch"), check_vma=False
    )
```
